256 devices in a mesh: head: 8 (over y, z_lo), tensor: 32 (over z_hi, x, core).
Axes of the slice: x: 4, y: 4, z: 8 (z_hi: 4, z_lo: 2; z = z_hi * 2 + z_lo), core: 2. Of those that a mesh axis runs over, the one named last changes fastest.
Arguments:
- tokens: bfloat16 [2048, 8192], P('head', 'tensor'), may hold values from -21 to 21
- w_query: bfloat16 [8192, 8192], P(None, 'tensor'), may hold values from -0.25 to 0.25
- w_key: bfloat16 [8192, 1024], P('tensor'), may hold values from -0.0625 to 0.0625
- w_value: bfloat16 [8192, 1024], P('tensor'), may hold values from -0.0625 to 0.0625
- w_out: bfloat16 [8192, 8192], P('tensor'), may hold values from -0.0625 to 0.0625
- down_query: bfloat16 [8, 8192, 64], P('head', 'tensor'), may hold values from -0.0625 to 0.0625
- up_query: bfloat16 [8, 64, 8192], P('head', None, 'tensor'), may hold values from -0.75 to 0.75
- down_key: bfloat16 [8, 8192, 64], P('head', 'tensor'), may hold values from -0.0625 to 0.0625
- up_key: bfloat16 [8, 64, 1024], P('head'), may hold values from -0.75 to 0.75
- down_value: bfloat16 [8, 8192, 64], P('head', 'tensor'), may hold values from -0.0625 to 0.0625
- up_value: bfloat16 [8, 64, 1024], P('head'), may hold values from -0.75 to 0.75
- down_out: bfloat16 [8, 8192, 64], P('head', 'tensor'), may hold values from -0.0625 to 0.0625
- up_out: bfloat16 [8, 64, 8192], P('head', None, 'tensor'), may hold values from -0.75 to 0.75
Outputs:
- layer_out: bfloat16 [2048, 8192], P('head', 'tensor')
The draws below stay inside these ranges and needn't reach their ends.
All inputs are finite; a program needn't handle non-finite values.
Results may differ from the reference program's by a relative error of at most 0.03.
Values may be sent and summed in bfloat16 or wider, within the bound.
No kernel may reach another device: no remote copies, remote signals or barrier semaphores. Data moves between devices by JAX's collectives and lax.ppermute only.
A program may use at most 128 MiB of HBM per device.

```python
import math
import jax
import jax.numpy as jnp
from jax import lax

D = 8192
QHEADS = 64
KVHEADS = 8
HEAD_DIM = 128
RANK = 64
TOK_DEV = 256
ADAPTER_COPIES = 8
KVW = 1024
TOKENS = 2048
N_HEAD = 8


def draw_tokens(key, part):
    key = jax.random.fold_in(key, 11)
    value_key = jax.random.fold_in(key, 0)
    values = jnp.clip(jax.random.normal(value_key, (TOKENS, D), jnp.float32), -6.0, 6.0)
    return values.astype(jnp.bfloat16)


def shard_levels(rng, dims, cuts, least, top_value):
    gain = 1.0
    for axis_at, shards_of in cuts:
        draws = jax.random.uniform(jax.random.fold_in(jax.random.fold_in(rng, 6), axis_at), (shards_of,), jnp.float32, least / len(cuts), top_value / len(cuts))
        gain = gain * jnp.repeat(jnp.exp(draws), dims[axis_at] // shards_of).reshape((-1,) + (1,) * (len(dims) - 1 - axis_at))
    return gain


def normal_values(rng, extent, spread, limit, pieces=(), held_as=jnp.bfloat16):
    values = jax.random.normal(rng, extent, jnp.float32) * spread
    if len(pieces) > 0:
        values = shard_levels(rng, extent, pieces, -0.22, 0.18) * values
    return jnp.clip(values, min=-limit, max=limit).astype(held_as)


def setup_inputs(seed: int = 0) -> dict:
    arg_keys = jax.random.split(jax.random.key(seed), 14)
    tokens = draw_tokens(jax.random.fold_in(arg_keys[13], 71), 0)
    w_query = normal_values(arg_keys[1], (D, D), (D // 16) ** -0.5, 0.25, ((1, 32),))
    w_key = normal_values(arg_keys[2], (D, KVW), D ** -0.5, 0.0625, ((0, 32),))
    w_value = normal_values(arg_keys[3], (D, KVW), D ** -0.5, 0.0625, ((0, 32),))
    w_out = normal_values(arg_keys[4], (D, D), D ** -0.5, 0.0625, ((0, 32),))
    down_query = normal_values(arg_keys[5], (ADAPTER_COPIES, D, RANK), D ** -0.5, 0.0625, ((0, 8), (1, 32)))
    up_query = normal_values(arg_keys[6], (ADAPTER_COPIES, RANK, D), RANK ** -0.5, 0.75, ((0, 8), (2, 32)))
    down_key = normal_values(arg_keys[7], (ADAPTER_COPIES, D, RANK), D ** -0.5, 0.0625, ((0, 8), (1, 32)))
    up_key = normal_values(arg_keys[8], (ADAPTER_COPIES, RANK, KVW), RANK ** -0.5, 0.75, ((0, 8),))
    down_value = normal_values(arg_keys[9], (ADAPTER_COPIES, D, RANK), D ** -0.5, 0.0625, ((0, 8), (1, 32)))
    up_value = normal_values(arg_keys[10], (ADAPTER_COPIES, RANK, KVW), RANK ** -0.5, 0.75, ((0, 8),))
    down_out = normal_values(arg_keys[11], (ADAPTER_COPIES, D, RANK), D ** -0.5, 0.0625, ((0, 8), (1, 32)))
    up_out = normal_values(arg_keys[12], (ADAPTER_COPIES, RANK, D), RANK ** -0.5, 0.75, ((0, 8), (2, 32)))
    return dict(tokens=tokens, w_query=w_query, w_key=w_key, w_value=w_value, w_out=w_out, down_query=down_query, up_query=up_query, down_key=down_key, up_key=up_key, down_value=down_value, up_value=up_value, down_out=down_out, up_out=up_out)


ADAPTER_SCALE = 2.0

def stack_down(down_stack):
    return jnp.transpose(down_stack, (1, 0, 2)).reshape(down_stack.shape[1], down_stack.shape[0] * down_stack.shape[2])

def stacked_up_factors(up_factor_stack):
    return up_factor_stack.reshape(up_factor_stack.shape[0] * up_factor_stack.shape[1], up_factor_stack.shape[2]).astype(jnp.float32)

def low_rank(inputs, down_stack, up_factor_stack):
    rank_reduced_rows = jnp.dot(inputs, stack_down(down_stack), preferred_element_type=jnp.float32)
    return jnp.dot(rank_reduced_rows, stacked_up_factors(up_factor_stack), precision=lax.Precision.HIGHEST) * (ADAPTER_SCALE / ADAPTER_COPIES)

def attend(seq_block):
    queries, key_states, value_states = seq_block
    group_size = QHEADS // KVHEADS
    query_heads = queries.reshape(TOK_DEV, QHEADS, HEAD_DIM).astype(jnp.float32)
    key_heads = jnp.repeat(key_states.reshape(TOK_DEV, KVHEADS, HEAD_DIM), group_size, axis=1).astype(jnp.float32)
    value_heads = jnp.repeat(value_states.reshape(TOK_DEV, KVHEADS, HEAD_DIM), group_size, axis=1).astype(jnp.float32)
    scores = jnp.einsum('qhd,khd->hqk', query_heads, key_heads, precision=lax.Precision.HIGHEST) * (1.0 / math.sqrt(HEAD_DIM))
    positions = jnp.arange(TOK_DEV, dtype=jnp.int32)
    causal = positions[:, None] >= positions[None, :]
    scores = jnp.where(causal[None], scores, -jnp.inf)
    row_max = lax.optimization_barrier(jnp.max(scores, axis=-1, keepdims=True))
    weights = jnp.exp(scores - row_max)
    probabilities = (weights / lax.optimization_barrier(jnp.sum(weights, axis=-1, keepdims=True))).astype(jnp.bfloat16)
    attended = jnp.einsum('hqk,khd->qhd', probabilities.astype(jnp.float32), value_heads, precision=lax.Precision.HIGHEST)
    return attended.astype(jnp.bfloat16).reshape(TOK_DEV, D)

def reference(tokens, w_query, w_key, w_value, w_out, down_query, up_query, down_key, up_key, down_value, up_value, down_out, up_out):
    queries = (jnp.dot(tokens, w_query, preferred_element_type=jnp.float32) + low_rank(tokens, down_query, up_query)).astype(jnp.bfloat16)
    key_states = (jnp.dot(tokens, w_key, preferred_element_type=jnp.float32) + low_rank(tokens, down_key, up_key)).astype(jnp.bfloat16)
    value_states = (jnp.dot(tokens, w_value, preferred_element_type=jnp.float32) + low_rank(tokens, down_value, up_value)).astype(jnp.bfloat16)
    attended = lax.map(attend, (queries.reshape(N_HEAD, TOK_DEV, D), key_states.reshape(N_HEAD, TOK_DEV, KVW), value_states.reshape(N_HEAD, TOK_DEV, KVW)))
    attended = attended.reshape(TOKENS, D)
    layer_out = jnp.dot(attended, w_out, preferred_element_type=jnp.float32) + low_rank(attended, down_out, up_out)
    return layer_out.astype(jnp.bfloat16)
```

```python
import functools
import math

import jax
import jax.numpy as jnp
from jax import lax
from jax.experimental import pallas as pl
from jax.experimental.pallas import tpu as pltpu
from jax.sharding import PartitionSpec as P

HEAD_DIM = 128
ADAPTER_SCALE = 2.0
NZ, NX, NC = 4, 4, 2
NH = 8
BF = jnp.bfloat16
F32 = jnp.float32


def tensor_perm(dz, dx, dc):
    pairs = []
    for t in range(NZ * NX * NC):
        z, x, c = t // (NX * NC), (t // NC) % NX, t % NC
        to = (((z - dz) % NZ) * NX + (x - dx) % NX) * NC + (c ^ dc)
        pairs.append((t, to))
    return pairs


def from_core(a):
    return lax.ppermute(a, "tensor", tensor_perm(0, 0, 1))


def from_x(a, d):
    return lax.ppermute(a, "tensor", tensor_perm(0, d, 0))


def from_z(a, d):
    return lax.ppermute(a, "tensor", tensor_perm(d, 0, 0))


def from_head(a, d):
    return lax.ppermute(a, "head", [(h, (h - d) % NH) for h in range(NH)])


def pick(a, index, axis):
    return lax.dynamic_index_in_dim(a, index, axis, keepdims=False)


def dot(a, b):
    return jnp.dot(a, b, preferred_element_type=F32)


def dot_t(a, b):
    return lax.dot_general(a, b, (((1,), (1,)), ((), ())), preferred_element_type=F32)


def roll_front(a, shift):
    n = a.shape[0]
    return lax.dynamic_slice_in_dim(jnp.concatenate([a, a], axis=0), shift, n, 0)


def attend_kernel(scale, q_mine, q_sib, rank, up_q, up_kv, k_base, v_base, out):
    ranks = up_q.shape[0]
    rq = rank[:, :ranks]
    rk = rank[:, ranks : 2 * ranks]
    rv = rank[:, 2 * ranks :]
    q = q_mine[...] + q_sib[...].astype(F32) + dot(rq, up_q[...]) * scale
    q = q.astype(BF)
    k = (k_base[...].astype(F32) + dot(rk, up_kv[:, :HEAD_DIM]) * scale).astype(BF)
    v = (v_base[...].astype(F32) + dot(rv, up_kv[:, HEAD_DIM:]) * scale).astype(BF)
    rows = q.shape[0]
    causal = lax.broadcasted_iota(jnp.int32, (rows, rows), 0) >= lax.broadcasted_iota(
        jnp.int32, (rows, rows), 1
    )
    for head in range(q.shape[1] // HEAD_DIM):
        cols = slice(head * HEAD_DIM, (head + 1) * HEAD_DIM)
        scores = dot_t(q[:, cols], k) * (1.0 / math.sqrt(HEAD_DIM))
        scores = jnp.where(causal, scores, -jnp.inf)
        weights = jnp.exp(scores - jnp.max(scores, axis=-1, keepdims=True))
        probs = (weights / jnp.sum(weights, axis=-1, keepdims=True)).astype(BF)
        out[:, cols] = dot(probs, v).astype(BF)


def attend(scale, q_mine, q_sib, rank, up_q, up_kv, k_base, v_base):
    return pl.pallas_call(
        functools.partial(attend_kernel, scale),
        out_shape=jax.ShapeDtypeStruct(q_mine.shape, BF),
        in_specs=[pl.BlockSpec(memory_space=pltpu.VMEM)] * 7,
        out_specs=pl.BlockSpec(memory_space=pltpu.VMEM),
        compiler_params=pltpu.CompilerParams(vmem_limit_bytes=32 * 2**20),
        cost_estimate=pl.CostEstimate(flops=400_000_000, bytes_accessed=3_000_000, transcendentals=131072),
    )(q_mine, q_sib, rank, up_q, up_kv, k_base, v_base)


def body(
    tokens,
    w_query,
    w_key,
    w_value,
    w_out,
    down_query,
    up_query,
    down_key,
    up_key,
    down_value,
    up_value,
    down_out,
    up_out,
):
    scale = ADAPTER_SCALE / NH
    h = lax.axis_index("head")
    t = lax.axis_index("tensor")
    c = t % NC
    x = (t // NC) % NX
    z = t // (NX * NC)
    rows, feats = tokens.shape

    downs = jnp.concatenate([down_query[0].T, down_key[0].T, down_value[0].T], axis=0)
    rank1 = down_query.shape[2]
    down_all = [downs] + [from_head(downs, d) for d in range(1, NH)]

    g = t // 4
    up_kv = jnp.concatenate(
        [
            lax.dynamic_slice_in_dim(up_key[0], g * HEAD_DIM, HEAD_DIM, 1),
            lax.dynamic_slice_in_dim(up_value[0], g * HEAD_DIM, HEAD_DIM, 1),
        ],
        axis=1,
    )
    late = jnp.concatenate([up_query[0], up_kv, down_out[0].T], axis=0)[None]
    late_all = lax.all_gather(late, "head", axis=0, tiled=True)
    up_out_z = jnp.concatenate([up_out] + [from_z(up_out[0], d)[None] for d in (1, 2, 3)], axis=0)
    up_out_all = lax.all_gather(up_out_z[None], "head", axis=0, tiled=True)

    tok_sib = from_core(tokens)

    is_key = c == 0
    w_kv_mine = jnp.where(is_key, w_key, w_value)
    w_kv_sib = from_core(jnp.where(is_key, w_value, w_key))
    kv_part = (dot(tokens, w_kv_mine) + dot(tok_sib, w_kv_sib)).astype(BF)
    kv_part = kv_part.reshape(rows, NZ, 2, HEAD_DIM)

    def kv_for(dest_x):
        return pick(kv_part, dest_x // 2, 2).reshape(rows, NZ * HEAD_DIM)

    kv_x = kv_for(x).astype(F32)
    for d in (1, 2, 3):
        kv_x = kv_x + from_x(kv_for((x - d) % NX), d).astype(F32)
    kv_x = kv_x.astype(BF).reshape(rows, NZ, HEAD_DIM)
    kv = pick(kv_x, z, 1).astype(F32)
    for d in (1, 2, 3):
        kv = kv + from_z(pick(kv_x, (z - d) % NZ, 1), d).astype(F32)
    kv = kv.astype(BF)
    kv_sib = from_core(kv)
    k_base = jnp.where(is_key, kv, kv_sib)
    v_base = jnp.where(is_key, kv_sib, kv)

    down_stack = jnp.stack([a.reshape(3, rank1, feats) for a in down_all], axis=1)
    down_stack = down_stack.reshape(3 * NH * rank1, feats)
    rank_part = dot_t(tokens, down_stack)
    half = rows // NC
    rank_part = rank_part.reshape(NC, half, 3 * NH * rank1)
    rank_half = pick(rank_part, c, 0) + from_core(pick(rank_part, 1 - c, 0).astype(BF)).astype(F32)
    rank_half = rank_half.astype(BF).reshape(NX, half // NX, 3 * NH * rank1)
    piece = pick(rank_half, x, 0).astype(F32)
    for d in (1, 2, 3):
        piece = piece + from_x(pick(rank_half, (x - d) % NX, 0), d).astype(F32)
    piece = piece.astype(BF)
    total = piece.astype(F32)
    for d in (1, 2, 3):
        total = total + from_z(piece, d).astype(F32)
    piece = total.astype(BF)
    pieces = jnp.stack([piece] + [from_x(piece, d) for d in (1, 2, 3)], axis=0)
    pieces = roll_front(pieces, (NX - x) % NX).reshape(half, 3 * NH * rank1)
    pieces_sib = from_core(pieces)
    rank_rows = jnp.where(
        is_key,
        jnp.concatenate([pieces, pieces_sib], axis=0),
        jnp.concatenate([pieces_sib, pieces], axis=0),
    )

    tok_z = jnp.concatenate([tokens] + [from_z(tokens, d) for d in (1, 2, 3)], axis=1)
    w_q = w_query.reshape(NZ, NX, NC, feats, feats)
    w_q_mine = pick(w_q, c, 2)
    w_q_sib = from_core(pick(w_q, 1 - c, 2))
    w_q_all = roll_front(jnp.concatenate([w_q_mine, w_q_sib], axis=3), z)

    def w_q_for(src_x):
        return pick(w_q_all, src_x, 1).reshape(NZ * feats, 2 * feats)

    q_part = dot(tok_z, w_q_for(x))
    for d in (1, 2, 3):
        q_part = q_part + dot(from_x(tok_z, d), w_q_for((x + d) % NX))
    q_sib = from_core(q_part[:, feats:])

    late_all = roll_front(late_all, h)
    up_q_all = late_all[:, :rank1].reshape(NH * rank1, feats)
    up_kv_all = late_all[:, rank1 : 2 * rank1].reshape(NH * rank1, feats)
    attended = attend(scale, q_part[:, :feats], q_sib, rank_rows, up_q_all, up_kv_all, k_base, v_base)

    att_chip = jnp.concatenate([attended, from_core(attended)], axis=1)
    w_o = w_out.reshape(feats, NZ, NX, NC, feats)
    w_o_chip = jnp.concatenate([pick(w_o, c, 3), from_core(pick(w_o, 1 - c, 3))], axis=0)
    down_o = late_all[:, 2 * rank1 :].reshape(NC, NH // 2 * rank1, feats)
    down_o_chip = jnp.concatenate([pick(down_o, c, 0), from_core(pick(down_o, 1 - c, 0))], axis=1)
    rank_o = dot_t(att_chip, down_o_chip)

    def out_for(dest_x):
        return dot(att_chip, pick(w_o_chip, dest_x, 2).reshape(2 * feats, NZ * feats))

    out_x = jnp.concatenate([out_for(x), rank_o], axis=1)
    rank_o = rank_o.astype(BF)
    for d in (2, 1, 3):
        send = jnp.concatenate([out_for((x - d) % NX).astype(BF), rank_o], axis=1)
        out_x = out_x + from_x(send, d).astype(F32)
    rank_mine = out_x[:, NZ * feats :].astype(BF)
    rank_sib = from_core(rank_mine)
    up_o = roll_front(up_out_all, h).transpose(0, 2, 1, 3).reshape(NC, NH // 2 * rank1, NZ * feats)
    low = dot(rank_mine, pick(up_o, c, 0)) + dot(rank_sib, pick(up_o, 1 - c, 0))

    out_x = roll_front(out_x[:, : NZ * feats].reshape(rows, NZ, feats).transpose(1, 0, 2), z)
    out_x = out_x + low.reshape(rows, NZ, feats).transpose(1, 0, 2) * scale
    out = out_x[0]
    for d in (2, 1, 3):
        out = out + from_z(out_x[NZ - d].astype(BF), d).astype(F32)
    return out.astype(BF)


def solution(mesh):
    placed = (
        P("head", "tensor"),
        P(None, "tensor"),
        P("tensor", None),
        P("tensor", None),
        P("tensor", None),
        P("head", "tensor", None),
        P("head", None, "tensor"),
        P("head", "tensor", None),
        P("head", None, None),
        P("head", "tensor", None),
        P("head", None, None),
        P("head", "tensor", None),
        P("head", None, "tensor"),
    )
    return jax.shard_map(
        body, mesh=mesh, in_specs=placed, out_specs=P("head", "tensor"), check_vma=False
    )
```

```python
import functools
import math

import jax
import jax.numpy as jnp
from jax import lax
from jax.experimental import pallas as pl
from jax.experimental.pallas import tpu as pltpu
from jax.sharding import PartitionSpec as P

HEAD_DIM = 128
ADAPTER_SCALE = 2.0
NZ, NX, NC = 4, 4, 2
NH = 8
RANK = 64
SCALE = ADAPTER_SCALE / NH
BF = jnp.bfloat16
F32 = jnp.float32
VMEM = pl.BlockSpec(memory_space=pltpu.VMEM)
SMEM = pl.BlockSpec(memory_space=pltpu.SMEM)


def tensor_perm(dz, dx, dc):
    pairs = []
    for t in range(NZ * NX * NC):
        z, x, c = t // (NX * NC), (t // NC) % NX, t % NC
        to = (((z - dz) % NZ) * NX + (x - dx) % NX) * NC + (c ^ dc)
        pairs.append((t, to))
    return pairs


def from_core(a):
    return lax.ppermute(a, "tensor", tensor_perm(0, 0, 1))


def from_x(a, d):
    return lax.ppermute(a, "tensor", tensor_perm(0, d, 0))


def from_z(a, d):
    return lax.ppermute(a, "tensor", tensor_perm(d, 0, 0))


def from_head(a, d):
    return lax.ppermute(a, "head", [(h, (h - d) % NH) for h in range(NH)])


def dot(a, b):
    return jnp.dot(a, b, preferred_element_type=F32)


def dot_t(a, b):
    return lax.dot_general(a, b, (((1,), (1,)), ((), ())), preferred_element_type=F32)


def at(start, size, unit=128):
    return pl.ds(pl.multiple_of(start, unit), size)


def struct(shape, dtype):
    return jax.ShapeDtypeStruct(shape, dtype)


def call(kernel, out_shape, args, scratch=(), flops=50_000_000, mib=16):
    size = sum(math.prod(a.shape) * a.dtype.itemsize for a in args)
    return pl.pallas_call(
        kernel,
        out_shape=out_shape,
        in_specs=[SMEM] + [VMEM] * (len(args) - 1),
        out_specs=jax.tree.map(lambda _: VMEM, out_shape),
        scratch_shapes=list(scratch),
        compiler_params=pltpu.CompilerParams(vmem_limit_bytes=mib * 2**20),
        cost_estimate=pl.CostEstimate(flops=flops, bytes_accessed=size, transcendentals=0),
    )(*args)


def pack_kernel(pos, dq, dk, dv, do, uq, uk, uv, uo, downs, late):
    g = pos[2] * 2 + pos[1] // 2
    downs[:RANK, :] = dq[0].T
    downs[RANK : 2 * RANK, :] = dk[0].T
    downs[2 * RANK :, :] = dv[0].T
    late[:RANK, :] = uq[0]
    cols = at(g * HEAD_DIM, HEAD_DIM)
    late[RANK : 2 * RANK, :HEAD_DIM] = uk[0, :, cols]
    late[RANK : 2 * RANK, HEAD_DIM:] = uv[0, :, cols]
    late[2 * RANK : 3 * RANK, :] = do[0].T
    late[3 * RANK :, :] = uo[0]


def kv_kernel(pos, tokens, tok_sib, wk, wv, wk_sib, wv_sib, own, s1, s2, s3, both):
    x, c = pos[1], pos[3]
    half, width = tok_sib.shape[0], wk.shape[1]
    mine = tokens[at(c * half, half), :]
    both[:, :width] = dot(mine, wk[...]) + dot(tok_sib[...], wk_sib[...])
    both[:, width:] = dot(mine, wv[...]) + dot(tok_sib[...], wv_sib[...])
    for d, out in enumerate((own, s1, s2, s3)):
        xh = lax.rem(x + NX - d, NX) // 2
        for zz in range(NZ):
            col = (2 * zz + xh) * HEAD_DIM
            base = zz * 2 * HEAD_DIM
            out[:, base : base + HEAD_DIM] = both[:, at(col, HEAD_DIM)].astype(out.dtype)
            out[:, base + HEAD_DIM : base + 2 * HEAD_DIM] = both[
                :, at(width + col, HEAD_DIM)
            ].astype(out.dtype)


def rank_kernel(pos, tokens, *refs):
    downs, (mine, send, stack) = refs[:NH], refs[NH:]
    c = pos[3]
    half = mine.shape[0]
    for d, down in enumerate(downs):
        for p in range(3):
            row = (p * NH + d) * RANK
            stack[row : row + RANK, :] = down[p * RANK : (p + 1) * RANK, :]
    mine[...] = dot_t(tokens[at(c * half, half), :], stack[...])
    send[...] = dot_t(tokens[at((1 - c) * half, half), :], stack[...]).astype(BF)


def rank_split_kernel(pos, mine, recv, own, s1, s2, s3, total):
    x = pos[1]
    total[...] = mine[...] + recv[...].astype(F32)
    width = own.shape[1]
    for d, out in enumerate((own, s1, s2, s3)):
        out[...] = total[:, at(lax.rem(x + NX - d, NX) * width, width)].astype(out.dtype)


def middle_kernel(pos, r0, r1, r2, r3, k0, k1, k2, k3, own, s1, s2, s3, kv):
    z = pos[2]
    rank = r0[...] + r1[...].astype(F32) + r2[...].astype(F32) + r3[...].astype(F32)
    kv[...] = k0[...] + k1[...].astype(F32) + k2[...].astype(F32) + k3[...].astype(F32)
    width = rank.shape[1]
    for d, out in enumerate((own, s1, s2, s3)):
        out[:, :width] = rank.astype(out.dtype)
        block = lax.rem(z + NZ - d, NZ) * 2 * HEAD_DIM
        out[:, width:] = kv[:, at(block, 2 * HEAD_DIM)].astype(out.dtype)


def rank_sum_kernel(pos, a0, a1, a2, a3, piece, kv):
    total = a0[...] + a1[...].astype(F32) + a2[...].astype(F32) + a3[...].astype(F32)
    width = piece.shape[1]
    piece[...] = total[:, :width].astype(BF)
    kv[...] = total[:, width:]


def gather_ranks(pos, pieces, rank):
    x = pos[1]
    for d, piece in enumerate(pieces):
        width = piece.shape[1]
        rank[:, at(lax.rem(x + d, NX) * width, width)] = piece[...]


def kv_final_kernel(pos, p0, p1, p2, p3, kv, late, out, rank, up):
    h = pos[0]
    gather_ranks(pos, (p0, p1, p2, p3), rank)
    n = NH * RANK
    for d in range(NH):
        up[d * RANK : (d + 1) * RANK, :] = late[lax.rem(h + d, NH), RANK : 2 * RANK, :]
    low_k = dot(rank[:, n : 2 * n], up[:, :HEAD_DIM])
    low_v = dot(rank[:, 2 * n :], up[:, HEAD_DIM:])
    out[:, :HEAD_DIM] = (kv[:, :HEAD_DIM] + low_k * SCALE).astype(BF)
    out[:, HEAD_DIM:] = (kv[:, HEAD_DIM:] + low_v * SCALE).astype(BF)


def attend_kernel(
    pos, p0, p1, p2, p3, q_mine, q_recv, late, late_sib, kv_mine, kv_recv, out, rank, up, kv, q
):
    h, c = pos[0], pos[3]
    gather_ranks(pos, (p0, p1, p2, p3), rank)
    n = NH * RANK
    feats = late.shape[2]
    half = q.shape[0]
    for d in range(NH):
        a = lax.rem(h + d, NH)
        up[d * RANK : (d + 1) * RANK, :feats] = late[a, :RANK, :]
        up[d * RANK : (d + 1) * RANK, feats:] = late_sib[a, :RANK, :]
    low = dot(rank[:, :n], up[...]) * SCALE
    q[:, :feats] = (q_mine[:, :feats] + q_recv[:, feats:] + low[:, :feats]).astype(BF)
    q[:, feats:] = (q_mine[:, feats:] + q_recv[:, :feats] + low[:, feats:]).astype(BF)
    kv[at(c * half, half), :] = kv_mine[...]
    kv[at((1 - c) * half, half), :] = kv_recv[...]
    k, v = kv[:, :HEAD_DIM], kv[:, HEAD_DIM:]
    rows = lax.broadcasted_iota(jnp.int32, (half, 2 * half), 0) + c * half
    causal = rows >= lax.broadcasted_iota(jnp.int32, (half, 2 * half), 1)
    for head in range(2 * feats // HEAD_DIM):
        cols = slice(head * HEAD_DIM, (head + 1) * HEAD_DIM)
        scores = dot_t(q[:, cols], k) * (1.0 / math.sqrt(HEAD_DIM))
        scores = jnp.where(causal, scores, -jnp.inf)
        weights = jnp.exp(scores - jnp.max(scores, axis=-1, keepdims=True))
        probs = (weights / jnp.sum(weights, axis=-1, keepdims=True)).astype(BF)
        out[:, cols] = dot(probs, v).astype(BF)


def stack_kernel(pos, a0, a1, a2, a3, out):
    for i, a in enumerate((a0, a1, a2, a3)):
        out[i] = a[...]


def parity_kernel(pos, w, out, sem):
    copy = pltpu.make_async_copy(w.at[:, 1 - pos[3]], out, sem)
    copy.start()
    copy.wait()


def other_parity(pos, w):
    n, _, rows, cols = w.shape
    return pl.pallas_call(
        parity_kernel,
        out_shape=struct((n, rows, cols), BF),
        in_specs=[SMEM, pl.BlockSpec(memory_space=pl.ANY)],
        out_specs=pl.BlockSpec(memory_space=pl.ANY),
        scratch_shapes=[pltpu.SemaphoreType.DMA],
        cost_estimate=pl.CostEstimate(flops=0, bytes_accessed=2 * n * rows * cols * 2, transcendentals=0),
    )(pos, w)


def query_kernel(pos, t0, t1, t2, t3, w, w_sib, mine, send, total):
    z, c = pos[2], pos[3]
    step = pl.program_id(0)
    feats = w.shape[3]

    @pl.when(step == 0)
    def _():
        total[...] = jnp.zeros_like(total)

    for d, tok in enumerate((t0, t1, t2, t3)):

        @pl.when(step == d)
        def _():
            left = total[:, :feats]
            right = total[:, feats:]
            for i in range(NZ):
                zz = lax.rem(z + i, NZ)
                left = left + dot(tok[i], w[zz, 0, 0])
                right = right + dot(tok[i], w_sib[zz, 0])
            total[:, :feats] = left
            total[:, feats:] = right

    @pl.when(step == NX - 1)
    def _():
        half = mine.shape[0]
        mine[...] = total[at(c * half, half), :]
        send[...] = total[at((1 - c) * half, half), :]


def query(pos, toks, w_query, w_sib):
    rows, feats = toks[0].shape[1:]
    half = rows // NC
    whole = lambda *shape: pl.BlockSpec(shape, lambda d, pos: (0,) * len(shape))
    return pl.pallas_call(
        query_kernel,
        grid_spec=pltpu.PrefetchScalarGridSpec(
            num_scalar_prefetch=1,
            grid=(NX,),
            in_specs=[whole(NZ, rows, feats)] * 4
            + [
                pl.BlockSpec(
                    (NZ, 1, 1, feats, feats),
                    lambda d, pos: (0, lax.rem(pos[1] + d, NX), pos[3], 0, 0),
                ),
                pl.BlockSpec(
                    (NZ, 1, feats, feats), lambda d, pos: (0, lax.rem(pos[1] + d, NX), 0, 0)
                ),
            ],
            out_specs=[whole(half, 2 * feats)] * 2,
            scratch_shapes=[pltpu.VMEM((rows, 2 * feats), F32)],
        ),
        out_shape=[struct((half, 2 * feats), F32)] * 2,
        compiler_params=pltpu.CompilerParams(vmem_limit_bytes=16 * 2**20),
        cost_estimate=pl.CostEstimate(flops=1_000_000_000, bytes_accessed=6_000_000, transcendentals=0),
    )(pos, *toks, w_query, w_sib)


def out_kernel(pos, att, w, w_sib, late, late_sib, out):
    step = pl.program_id(0)
    feats = w.shape[0]
    mine, sib = att[:, :feats], att[:, feats:]

    @pl.when(step < NZ)
    def _():
        out[...] = (dot(mine, w[...]) + dot(sib, w_sib[...])).astype(out.dtype)

    @pl.when(step == NZ)
    def _():
        n = NH * RANK
        down = late[...].reshape(n, feats)
        down_sib = late_sib[...].reshape(n, feats)
        out[...] = (dot_t(mine, down) + dot_t(sib, down_sib)).astype(out.dtype)


def out_partial(pos, d, att, w_out, w_sib, late, late_sib):
    half = att.shape[0]
    feats = w_out.shape[0]
    width = NC * feats
    weights = pl.BlockSpec(
        (feats, width),
        lambda s, pos: (0, jnp.minimum(s, NZ - 1) * NX + lax.rem(pos[1] + NX - d, NX)),
    )
    factors = pl.BlockSpec((NH, RANK, feats), lambda s, pos: (0, 2, 0))
    return pl.pallas_call(
        out_kernel,
        grid_spec=pltpu.PrefetchScalarGridSpec(
            num_scalar_prefetch=1,
            grid=(NZ + 1,),
            in_specs=[
                pl.BlockSpec(att.shape, lambda s, pos: (0, 0)),
                weights,
                weights,
                factors,
                factors,
            ],
            out_specs=pl.BlockSpec((half, width), lambda s, pos: (0, s)),
        ),
        out_shape=struct((half, (NZ + 1) * width), F32 if d == 0 else BF),
        compiler_params=pltpu.CompilerParams(vmem_limit_bytes=16 * 2**20),
        cost_estimate=pl.CostEstimate(flops=330_000_000, bytes_accessed=3_300_000, transcendentals=0),
    )(pos, att, w_out, w_sib, late, late_sib)


def out_middle_kernel(pos, a0, a1, a2, a3, *refs):
    ups, (own, s1, s2, s3, low) = refs[:8], refs[8:]
    z, c = pos[2], pos[3]
    width = own.shape[1]
    feats = width // NC
    n = NH * RANK

    def total(cols):
        return (
            a0[:, cols]
            + a1[:, cols].astype(F32)
            + a2[:, cols].astype(F32)
            + a3[:, cols].astype(F32)
        )

    rank = total(slice(NZ * width, (NZ + 1) * width)).astype(BF)
    for d, out in enumerate((own, s1, s2, s3)):
        e = (NZ - d) % NZ
        low[:, at(c * feats, feats)] = dot(rank, ups[e][...].reshape(n, feats))
        low[:, at((1 - c) * feats, feats)] = dot(rank, ups[4 + e][...].reshape(n, feats))
        block = at(lax.rem(z + NZ - d, NZ) * width, width)
        out[...] = (total(block) + low[...] * SCALE).astype(out.dtype)


def final_kernel(pos, a0, a1, a2, a3, mine, send, total):
    c = pos[3]
    feats = mine.shape[1]
    total[...] = a0[...] + a1[...].astype(F32) + a2[...].astype(F32) + a3[...].astype(F32)
    mine[...] = total[:, at(c * feats, feats)].astype(BF)
    send[...] = total[:, at((1 - c) * feats, feats)].astype(BF)


def join_kernel(pos, mine, recv, out):
    c = pos[3]
    half = mine.shape[0]
    out[at(c * half, half), :] = mine[...]
    out[at((1 - c) * half, half), :] = recv[...]


def body(
    tokens,
    w_query,
    w_key,
    w_value,
    w_out,
    down_query,
    up_query,
    down_key,
    up_key,
    down_value,
    up_value,
    down_out,
    up_out,
):
    h = lax.axis_index("head")
    t = lax.axis_index("tensor")
    c = t % NC
    x = (t // NC) % NX
    z = t // (NX * NC)
    pos = jnp.stack([h, x, z, c]).astype(jnp.int32)
    rows, feats = tokens.shape
    half = rows // NC
    n = NH * RANK
    vm = pltpu.VMEM

    def four(shape):
        return [struct(shape, F32)] + [struct(shape, BF)] * 3

    downs, late = call(
        pack_kernel,
        [struct((3 * RANK, feats), BF), struct((4 * RANK, feats), BF)],
        (pos, down_query, down_key, down_value, down_out, up_query, up_key, up_value, up_out),
    )
    late_all = lax.all_gather(late[None], "head", axis=0, tiled=True)
    down_all = [downs] + [from_head(downs, d) for d in range(1, NH)]
    tok_sib = from_core(lax.dynamic_slice_in_dim(tokens, (1 - c) * half, half, 0))

    mine, send = call(
        rank_kernel,
        [struct((half, 3 * n), F32), struct((half, 3 * n), BF)],
        (pos, tokens, *down_all),
        [vm((3 * n, feats), BF)],
        flops=200_000_000,
    )
    own, *sends = call(
        rank_split_kernel,
        four((half, 3 * n // NX)),
        (pos, mine, from_core(send)),
        [vm((half, 3 * n), F32)],
    )
    rank_x = [own] + [from_x(s, d) for d, s in zip((1, 2, 3), sends)]

    own, *sends = call(
        kv_kernel,
        four((half, NZ * 2 * HEAD_DIM)),
        (pos, tokens, tok_sib, w_key, w_value, from_core(w_key), from_core(w_value)),
        [vm((half, 2 * w_key.shape[1]), F32)],
        flops=270_000_000,
    )
    kv_x = [own] + [from_x(s, d) for d, s in zip((1, 2, 3), sends)]

    own, *sends = call(
        middle_kernel,
        four((half, 3 * n // NX + 2 * HEAD_DIM)),
        (pos, *rank_x, *kv_x),
        [vm((half, NZ * 2 * HEAD_DIM), F32)],
    )
    both_z = [own] + [from_z(s, d) for d, s in zip((1, 2, 3), sends)]
    piece, kv_base = call(
        rank_sum_kernel,
        [struct((half, 3 * n // NX), BF), struct((half, 2 * HEAD_DIM), F32)],
        (pos, *both_z),
    )
    pieces = [piece] + [from_x(piece, d) for d in (1, 2, 3)]

    tok_z = call(
        stack_kernel,
        struct((NZ, rows, feats), BF),
        (pos, tokens, *[from_z(tokens, d) for d in (1, 2, 3)]),
    )
    tok_x = [tok_z] + [from_x(tok_z, d) for d in (1, 2, 3)]
    w_q_sib = from_core(other_parity(pos, w_query.reshape(NZ * NX, NC, feats, feats)))
    q_mine, q_send = query(
        pos,
        tok_x,
        w_query.reshape(NZ, NX, NC, feats, feats),
        w_q_sib.reshape(NZ, NX, feats, feats),
    )
    q_recv = from_core(q_send)

    late_sib = from_core(late_all)
    kv_mine = call(
        kv_final_kernel,
        struct((half, 2 * HEAD_DIM), BF),
        (pos, *pieces, kv_base, late_all),
        [vm((half, 3 * n), BF), vm((n, 2 * HEAD_DIM), BF)],
    )
    att = call(
        attend_kernel,
        struct((half, NC * feats), BF),
        (pos, *pieces, q_mine, q_recv, late_all, late_sib, kv_mine, from_core(kv_mine)),
        [
            vm((half, 3 * n), BF),
            vm((n, NC * feats), BF),
            vm((rows, 2 * HEAD_DIM), BF),
            vm((half, NC * feats), BF),
        ],
        flops=200_000_000,
    )

    up_o = late_all[:, 3 * RANK :]
    ups = [up_o] + [from_z(up_o, d) for d in (1, 2, 3)]
    ups = ups + [late_sib[:, 3 * RANK :]] + [from_core(u) for u in ups[1:]]
    w_o_sib = from_core(w_out)
    out_x = {
        d: out_partial(pos, d, att, w_out, w_o_sib, late_all, late_sib) for d in (2, 1, 3, 0)
    }
    out_x = [out_x[0]] + [from_x(out_x[d], d) for d in (1, 2, 3)]
    own, *sends = call(
        out_middle_kernel,
        four((half, NC * feats)),
        (pos, *out_x, *ups),
        [vm((half, NC * feats), F32)],
        flops=270_000_000,
    )
    out_z = [own] + [from_z(s, d) for d, s in zip((1, 2, 3), sends)]
    mine, send = call(
        final_kernel, [struct((half, feats), BF)] * 2, (pos, *out_z), [vm((half, NC * feats), F32)]
    )
    return call(join_kernel, struct((rows, feats), BF), (pos, mine, from_core(send)))


def solution(mesh):
    placed = (
        P("head", "tensor"),
        P(None, "tensor"),
        P("tensor", None),
        P("tensor", None),
        P("tensor", None),
        P("head", "tensor", None),
        P("head", None, "tensor"),
        P("head", "tensor", None),
        P("head", None, None),
        P("head", "tensor", None),
        P("head", None, None),
        P("head", "tensor", None),
        P("head", None, "tensor"),
    )
    return jax.shard_map(
        body, mesh=mesh, in_specs=placed, out_specs=P("head", "tensor"), check_vma=False
    )
```

```python
import functools
import math

import jax
import jax.numpy as jnp
from jax import lax
from jax.experimental import pallas as pl
from jax.experimental.pallas import tpu as pltpu
from jax.sharding import PartitionSpec as P

HEAD_DIM = 128
ADAPTER_SCALE = 2.0
NZ, NX, NC = 4, 4, 2
NH = 8
RANK = 64
SCALE = ADAPTER_SCALE / NH
BF = jnp.bfloat16
F32 = jnp.float32
VMEM = pl.BlockSpec(memory_space=pltpu.VMEM)
HBM = pl.BlockSpec(memory_space=pltpu.HBM)
TINY = pl.CostEstimate(flops=1000, bytes_accessed=1000, transcendentals=0)
SMEM = pl.BlockSpec(memory_space=pltpu.SMEM)


def tensor_perm(dz, dx, dc):
    pairs = []
    for t in range(NZ * NX * NC):
        z, x, c = t // (NX * NC), (t // NC) % NX, t % NC
        to = (((z - dz) % NZ) * NX + (x - dx) % NX) * NC + (c ^ dc)
        pairs.append((t, to))
    return pairs


def from_core(a):
    return lax.ppermute(a, "tensor", tensor_perm(0, 0, 1))


def from_x(a, d):
    return lax.ppermute(a, "tensor", tensor_perm(0, d, 0))


def from_z(a, d):
    return lax.ppermute(a, "tensor", tensor_perm(d, 0, 0))


def from_head(a, d):
    return lax.ppermute(a, "head", [(h, (h - d) % NH) for h in range(NH)])


def swap_all(a, axis, groups=None):
    return lax.all_to_all(a, axis, 0, 0, axis_index_groups=groups, tiled=True)


def tensor_groups(key):
    groups = {}
    for t in range(NZ * NX * NC):
        groups.setdefault(key(t // (NX * NC), (t // NC) % NX, t % NC), []).append(t)
    return list(groups.values())


def swap_x(a):
    return swap_all(a, "tensor", tensor_groups(lambda z, x, c: (z, c)))


def swap_z(a):
    return swap_all(a, "tensor", tensor_groups(lambda z, x, c: (x, c)))


def swap_xz(a):
    return swap_all(a, "tensor", tensor_groups(lambda z, x, c: c))


def dot(a, b):
    return jnp.dot(a, b, preferred_element_type=F32)


def dot_t(a, b):
    return lax.dot_general(a, b, (((1,), (1,)), ((), ())), preferred_element_type=F32)


def join(parts):
    width = sum(a.shape[-1] for a in parts)
    total, start = None, 0
    for a in parts:
        edges = [(0, 0, 0)] * (a.ndim - 1) + [(start, width - start - a.shape[-1], 0)]
        piece = lax.pad(a, jnp.zeros((), a.dtype), edges)
        total = piece if total is None else total + piece
        start += a.shape[-1]
    return total


def tie(*parts):
    return lax.optimization_barrier(parts)


def at(start, size, unit=128):
    return pl.ds(pl.multiple_of(start, unit), size)


def struct(shape, dtype):
    return jax.ShapeDtypeStruct(shape, dtype)


def fetching(kernel, held, *refs):
    refs, extra = list(refs[:-len(held) - 1]), refs[-len(held) - 1 :]
    buffers, sem = extra[:-1], extra[-1]
    copies = [
        pltpu.make_async_copy(refs[place], buffer, sem.at[i])
        for i, (place, buffer) in enumerate(zip(held, buffers))
    ]
    for copy in copies:
        copy.start()
    for copy in copies:
        copy.wait()
    for place, buffer in zip(held, buffers):
        refs[place] = buffer
    kernel(*refs)


def call(kernel, out_shape, args, scratch=(), held=(), mib=24):
    specs = [SMEM] + [HBM if i in held else VMEM for i in range(1, len(args))]
    scratch = list(scratch)
    if held:
        kernel = functools.partial(fetching, kernel, tuple(held))
        scratch += [pltpu.VMEM(args[i].shape, args[i].dtype) for i in held]
        scratch += [pltpu.SemaphoreType.DMA((len(held),))]
    return pl.pallas_call(
        kernel,
        out_shape=out_shape,
        in_specs=specs,
        out_specs=jax.tree.map(lambda _: VMEM, out_shape),
        scratch_shapes=scratch,
        compiler_params=pltpu.CompilerParams(vmem_limit_bytes=mib * 2**20),
        cost_estimate=TINY,
    )(*args)


PARTS = 7


def factor(packs, i):
    feats = packs.shape[2] // PARTS
    return packs[:, :, i * feats : (i + 1) * feats].reshape(NH * RANK, feats)


def kv_kernel(pos, tokens, tok_sib, wk, wv, wk_sib, wv_sib, own, s1, s2, s3, both):
    x, c = pos[1], pos[3]
    half, width = tok_sib.shape[0], wk.shape[1]
    mine = tokens[at(c * half, half), :]
    for i, (w, w_sib) in enumerate(((wk, wk_sib), (wv, wv_sib))):
        part = dot(mine, w[...]) + dot(tok_sib[...], w_sib[...])
        for g in range(width // HEAD_DIM):
            base = ((g % 2) * NZ * 2 + (g // 2) * 2 + i) * HEAD_DIM
            both[:, base : base + HEAD_DIM] = part[:, g * HEAD_DIM : (g + 1) * HEAD_DIM]
    for d, out in enumerate((own, s1, s2, s3)):
        xh = lax.rem(x + NX - d, NX) // 2
        out[...] = both[:, at(xh * width, width)].astype(out.dtype)


def kv_middle_kernel(pos, a0, a1, a2, a3, own, s1, s2, s3):
    z = pos[2]
    width = own.shape[1]
    for d, out in enumerate((own, s1, s2, s3)):
        cols = at(lax.rem(z + NZ - d, NZ) * width, width)
        total = a0[:, cols] + a1[:, cols].astype(F32)
        total = total + a2[:, cols].astype(F32) + a3[:, cols].astype(F32)
        out[...] = total.astype(out.dtype)


def rank_kernel(pos, tokens, packs, mine, send, stack):
    c = pos[3]
    half = mine.shape[0]
    feats = tokens.shape[1]
    for d in range(NH):
        for p in range(3):
            row = (p * NH + d) * RANK
            stack[row : row + RANK, :] = packs[d, :, p * feats : (p + 1) * feats]
    mine[...] = dot_t(tokens[at(c * half, half), :], stack[...])
    send[...] = dot_t(tokens[at((1 - c) * half, half), :], stack[...]).astype(BF)


def rank_split_kernel(pos, mine, recv, out):
    out[...] = (mine[...] + recv[...].astype(F32)).reshape(out.shape).astype(BF)


def rank_sum_kernel(pos, parts, out):
    total = parts[0].astype(F32)
    for i in range(1, NZ * NX):
        total = total + parts[i].astype(F32)
    for i in range(NZ * NX):
        out[i] = total.astype(BF)


def gather_ranks(pieces, cols):
    chips, rows, _ = pieces.shape
    part = pieces[:, :, cols].astype(F32)
    return part.reshape(chips * rows, part.shape[2]).astype(BF)


def kv_final_kernel(pos, pieces, a0, a1, a2, a3, early, out):
    n = NH * RANK
    up = factor(early, 4)
    kv = a0[...] + a1[...].astype(F32) + a2[...].astype(F32) + a3[...].astype(F32)
    low_k = dot(gather_ranks(pieces, slice(n, 2 * n)), up[:, :HEAD_DIM])
    low_v = dot(gather_ranks(pieces, slice(2 * n, 3 * n)), up[:, HEAD_DIM:])
    out[:, :HEAD_DIM] = (kv[:, :HEAD_DIM] + low_k * SCALE).astype(BF)
    out[:, HEAD_DIM:] = (kv[:, HEAD_DIM:] + low_v * SCALE).astype(BF)


def attend_kernel(
    pos, pieces, q_mine, q_recv, early, early_sib, kv_mine, kv_recv, out, kv, q
):
    c = pos[3]
    rank = gather_ranks(pieces, slice(0, NH * RANK))
    feats = early.shape[2] // PARTS
    half = q.shape[0]
    low = dot(rank, factor(early, 3)) * SCALE
    low_sib = dot(rank, factor(early_sib, 3)) * SCALE
    q[:, :feats] = (q_mine[...] + low).astype(BF)
    q[:, feats:] = (q_recv[...] + low_sib).astype(BF)
    kv[at(c * half, half), :] = kv_mine[...]
    kv[at((1 - c) * half, half), :] = kv_recv[...]
    k, v = kv[:, :HEAD_DIM], kv[:, HEAD_DIM:]
    rows = lax.broadcasted_iota(jnp.int32, (half, 2 * half), 0) + c * half
    causal = rows >= lax.broadcasted_iota(jnp.int32, (half, 2 * half), 1)
    for head in range(2 * feats // HEAD_DIM):
        cols = slice(head * HEAD_DIM, (head + 1) * HEAD_DIM)
        scores = dot_t(q[:, cols], k) * (1.0 / math.sqrt(HEAD_DIM))
        scores = jnp.where(causal, scores, -jnp.inf)
        weights = jnp.exp(scores - jnp.max(scores, axis=-1, keepdims=True))
        probs = (weights / jnp.sum(weights, axis=-1, keepdims=True)).astype(BF)
        out[:, cols] = dot(probs, v).astype(BF)


def query_kernel(pos, tok, w, mine, send, total):
    c = pos[3]
    step = pl.program_id(0)

    @pl.when(step == 0)
    def _():
        total[...] = jnp.zeros_like(total)

    part = dot(tok[0], w[0])
    for i in range(1, tok.shape[0]):
        part = part + dot(tok[i], w[i])
    total[...] += part

    @pl.when(step == pl.num_programs(0) - 1)
    def _():
        half = mine.shape[0]
        mine[...] = total[at(c * half, half), :]
        send[...] = total[at((1 - c) * half, half), :]


def query(pos, toks, w_query):
    blocks, rows, feats = toks.shape
    half = rows // NC
    steps = 4
    part = pl.BlockSpec((blocks // steps, rows, feats), lambda d, pos: (d, 0, 0))
    return pl.pallas_call(
        query_kernel,
        grid_spec=pltpu.PrefetchScalarGridSpec(
            num_scalar_prefetch=1,
            grid=(steps,),
            in_specs=[part, part],
            out_specs=[pl.BlockSpec((half, feats), lambda d, pos: (0, 0))] * 2,
            scratch_shapes=[pltpu.VMEM((rows, feats), F32)],
        ),
        out_shape=[struct((half, feats), F32)] * 2,
        compiler_params=pltpu.CompilerParams(vmem_limit_bytes=40 * 2**20),
        cost_estimate=TINY,
    )(pos, toks, w_query)


SPLIT = 4


def out_kernel(pos, att, w, w_sib, out, here, here_sib, sem):
    z = pos[2]
    blocks = NX * NZ
    width = att.shape[1]
    feats = width // NC
    part_rows = feats // SPLIT

    def fetch(k):
        cols = slice(k * width, (k + 1) * width)
        copies = []
        for j in range(SPLIT):
            rows = slice(j * part_rows, (j + 1) * part_rows)
            copies.append(pltpu.make_async_copy(w.at[rows, cols], here.at[k, rows], sem.at[2 * k]))
            copies.append(
                pltpu.make_async_copy(
                    w_sib.at[rows, cols], here_sib.at[k, rows], sem.at[2 * k + 1]
                )
            )
        return copies

    for k in range(blocks):
        for copy in fetch(k):
            copy.start()

    def step(k, carry):
        some = pl.ds(0, width)
        pltpu.make_async_copy(w.at[:, some], here.at[k], sem.at[2 * k]).wait()
        pltpu.make_async_copy(w_sib.at[:, some], here_sib.at[k], sem.at[2 * k + 1]).wait()
        part = dot(att[:, :feats], here[k]) + dot(att[:, feats:], here_sib[k])
        out[k % NX, lax.rem(k // NX + NZ - z, NZ)] = part.astype(out.dtype)
        return carry

    lax.fori_loop(0, blocks, step, 0)


def out_partial(pos, att, w_out, w_sib):
    half, width = att.shape
    feats = width // NC
    blocks = NX * NZ
    return pl.pallas_call(
        out_kernel,
        in_specs=[SMEM, VMEM, HBM, HBM],
        out_specs=VMEM,
        out_shape=struct((NX, NZ, half, width), BF),
        scratch_shapes=[pltpu.VMEM((blocks, feats, width), BF)] * 2
        + [pltpu.SemaphoreType.DMA((2 * blocks,))],
        compiler_params=pltpu.CompilerParams(vmem_limit_bytes=40 * 2**20),
        cost_estimate=TINY,
    )(pos, att, w_out, w_sib)


def out_rank_kernel(pos, att, early, early_sib, out):
    feats = early.shape[2] // PARTS
    rank = dot_t(att[:, :feats], factor(early, 5))
    rank = rank + dot_t(att[:, feats:], factor(early_sib, 5))
    for j in range(NZ):
        out[j] = rank.astype(BF)


def out_rank_sum_kernel(pos, a, out):
    total = a[0].astype(F32) + a[1].astype(F32) + a[2].astype(F32) + a[3].astype(F32)
    for j in range(NX):
        out[j] = total.astype(BF)


def final_kernel(pos, a0, a1, a2, a3, r, early, early_sib, mine, send):
    c = pos[3]
    feats = mine.shape[1]
    rank = r[0].astype(F32) + r[1].astype(F32) + r[2].astype(F32) + r[3].astype(F32)
    rank = rank.astype(BF)

    def total(cols):
        part = a0[:, cols].astype(F32) + a1[:, cols].astype(F32)
        return part + a2[:, cols].astype(F32) + a3[:, cols].astype(F32)

    low = dot(rank, factor(early, 6)) * SCALE
    low_sib = dot(rank, factor(early_sib, 6)) * SCALE
    mine[...] = (total(at(c * feats, feats)) + low).astype(BF)
    send[...] = (total(at((1 - c) * feats, feats)) + low_sib).astype(BF)


def join_kernel(pos, mine, recv, out):
    c = pos[3]
    half = mine.shape[0]
    out[at(c * half, half), :] = mine[...]
    out[at((1 - c) * half, half), :] = recv[...]


def body(
    tokens,
    w_query,
    w_key,
    w_value,
    w_out,
    down_query,
    up_query,
    down_key,
    up_key,
    down_value,
    up_value,
    down_out,
    up_out,
):
    h = lax.axis_index("head")
    t = lax.axis_index("tensor")
    c = t % NC
    x = (t // NC) % NX
    z = t // (NX * NC)
    pos = jnp.stack([h, x, z, c]).astype(jnp.int32)
    rows, feats = tokens.shape
    half = rows // NC
    n = NH * RANK
    vm = pltpu.VMEM
    x_groups = tensor_groups(lambda z, x, c: (z, c))

    def four(shape):
        return [struct(shape, F32)] + [struct(shape, BF)] * 3

    tok_zs = [tokens] + [from_z(tokens, d) for d in (1, 2, 3)]
    g = t // 4
    downs = [jnp.swapaxes(a, 1, 2) for a in (down_query, down_key, down_value, down_out)]
    up_kv = [lax.dynamic_slice_in_dim(a, g * HEAD_DIM, HEAD_DIM, 2) for a in (up_key, up_value)]
    early = join([*downs[:3], up_query, *up_kv, downs[3], up_out])
    early = swap_all(jnp.broadcast_to(early, (NH, *early.shape[1:])), "head")

    tok_all = lax.all_gather(tokens[None], "tensor", axis=0, tiled=True)

    tok_sib = from_core(lax.dynamic_slice_in_dim(tokens, (1 - c) * half, half, 0))
    own, *sends = call(
        kv_kernel,
        four((half, NZ * 2 * HEAD_DIM)),
        (pos, tokens, tok_sib, w_key, w_value, from_core(w_key), from_core(w_value)),
        [vm((half, 2 * w_key.shape[1]), F32)],
        held=(1, 3, 4),
    )
    kv_x = [own] + [from_x(s, d) for d, s in zip((1, 2, 3), sends)]
    early, kv_x = tie(early, kv_x)

    mine, send = call(
        rank_kernel,
        [struct((half, 3 * n), F32), struct((half, 3 * n), BF)],
        (pos, tokens, early),
        [vm((3 * n, feats), BF)],
        held=(1,),
    )
    chips = NZ * NX
    pieces = call(
        rank_split_kernel,
        struct((chips, half // chips, 3 * n), BF),
        (pos, mine, from_core(send)),
    )
    early_sib = from_core(early)
    own, *sends = call(kv_middle_kernel, four((half, 2 * HEAD_DIM)), (pos, *kv_x))
    kv_z = [own] + [from_z(s, d) for d, s in zip((1, 2, 3), sends)]
    pieces = swap_xz(pieces)
    pieces, early_sib, w_out_now, kv_z = tie(pieces, early_sib, w_out, kv_z)
    w_o_sib = from_core(w_out_now)
    pieces = call(rank_sum_kernel, struct(pieces.shape, BF), (pos, pieces))
    pieces = swap_xz(pieces)

    q_mine, q_send = query(pos, tok_all, w_query.reshape(NZ * NX * NC, feats, feats))
    q_recv = from_core(q_send)
    pieces, w_o_sib, q_recv = tie(pieces, w_o_sib, q_recv)
    kv_mine = call(kv_final_kernel, struct((half, 2 * HEAD_DIM), BF), (pos, pieces, *kv_z, early))

    att = call(
        attend_kernel,
        struct((half, NC * feats), BF),
        (pos, pieces, q_mine, q_recv, early, early_sib, kv_mine, from_core(kv_mine)),
        [vm((rows, 2 * HEAD_DIM), BF), vm((half, NC * feats), BF)],
    )

    rank_o = call(out_rank_kernel, struct((NZ, half, n), BF), (pos, att, early, early_sib))
    att, rank_o = tie(att, rank_o)
    out = out_partial(pos, att, w_out, w_o_sib)
    out_x = lax.psum_scatter(
        out, "tensor", scatter_dimension=0, tiled=True, axis_index_groups=x_groups
    )
    rank_o, _ = tie(rank_o, out)
    rank_o = call(out_rank_sum_kernel, struct((NX, half, n), BF), (pos, swap_z(rank_o)))
    rank_o = swap_x(rank_o)
    out_x = [out_x[0, i] for i in range(NZ)]
    out_z = [out_x[0]] + [from_z(out_x[NZ - d], d) for d in (1, 2, 3)]
    mine, send = call(
        final_kernel, [struct((half, feats), BF)] * 2, (pos, *out_z, rank_o, early, early_sib)
    )
    return call(join_kernel, struct((rows, feats), BF), (pos, mine, from_core(send)))


def solution(mesh):
    placed = (
        P("head", "tensor"),
        P(None, "tensor"),
        P("tensor", None),
        P("tensor", None),
        P("tensor", None),
        P("head", "tensor", None),
        P("head", None, "tensor"),
        P("head", "tensor", None),
        P("head", None, None),
        P("head", "tensor", None),
        P("head", None, None),
        P("head", "tensor", None),
        P("head", None, "tensor"),
    )
    return jax.shard_map(
        body, mesh=mesh, in_specs=placed, out_specs=P("head", "tensor"), check_vma=False
    )
```

```python
import functools
import math

import jax
import jax.numpy as jnp
from jax import lax
from jax.experimental import pallas as pl
from jax.experimental.pallas import tpu as pltpu
from jax.sharding import PartitionSpec as P

HEAD_DIM = 128
ADAPTER_SCALE = 2.0
NZ, NX, NC = 4, 4, 2
NH = 8
RANK = 64
SCALE = ADAPTER_SCALE / NH
BF = jnp.bfloat16
F32 = jnp.float32
VMEM = pl.BlockSpec(memory_space=pltpu.VMEM)
HBM = pl.BlockSpec(memory_space=pltpu.HBM)
TINY = pl.CostEstimate(flops=1000, bytes_accessed=1000, transcendentals=0)
SMEM = pl.BlockSpec(memory_space=pltpu.SMEM)


def tensor_perm(dz, dx, dc):
    pairs = []
    for t in range(NZ * NX * NC):
        z, x, c = t // (NX * NC), (t // NC) % NX, t % NC
        to = (((z - dz) % NZ) * NX + (x - dx) % NX) * NC + (c ^ dc)
        pairs.append((t, to))
    return pairs


def from_core(a):
    return lax.ppermute(a, "tensor", tensor_perm(0, 0, 1))


def from_x(a, d):
    return lax.ppermute(a, "tensor", tensor_perm(0, d, 0))


def from_z(a, d):
    return lax.ppermute(a, "tensor", tensor_perm(d, 0, 0))


def from_head(a, d):
    return lax.ppermute(a, "head", [(h, (h - d) % NH) for h in range(NH)])


def swap_all(a, axis, groups=None):
    return lax.all_to_all(a, axis, 0, 0, axis_index_groups=groups, tiled=True)


def tensor_groups(key):
    groups = {}
    for t in range(NZ * NX * NC):
        groups.setdefault(key(t // (NX * NC), (t // NC) % NX, t % NC), []).append(t)
    return list(groups.values())


def swap_x(a):
    return swap_all(a, "tensor", tensor_groups(lambda z, x, c: (z, c)))


def swap_z(a):
    return swap_all(a, "tensor", tensor_groups(lambda z, x, c: (x, c)))


def swap_xz(a):
    return swap_all(a, "tensor", tensor_groups(lambda z, x, c: c))


def dot(a, b):
    return jnp.dot(a, b, preferred_element_type=F32)


def dot_t(a, b):
    return lax.dot_general(a, b, (((1,), (1,)), ((), ())), preferred_element_type=F32)


def join(parts):
    width = sum(a.shape[-1] for a in parts)
    total, start = None, 0
    for a in parts:
        edges = [(0, 0, 0)] * (a.ndim - 1) + [(start, width - start - a.shape[-1], 0)]
        piece = lax.pad(a, jnp.zeros((), a.dtype), edges)
        total = piece if total is None else total + piece
        start += a.shape[-1]
    return total


def tie(*parts):
    return lax.optimization_barrier(parts)


def at(start, size, unit=128):
    return pl.ds(pl.multiple_of(start, unit), size)


def struct(shape, dtype):
    return jax.ShapeDtypeStruct(shape, dtype)


def fetching(kernel, held, *refs):
    refs, extra = list(refs[:-len(held) - 1]), refs[-len(held) - 1 :]
    buffers, sem = extra[:-1], extra[-1]
    copies = [
        pltpu.make_async_copy(refs[place], buffer, sem.at[i])
        for i, (place, buffer) in enumerate(zip(held, buffers))
    ]
    for copy in copies:
        copy.start()
    for copy in copies:
        copy.wait()
    for place, buffer in zip(held, buffers):
        refs[place] = buffer
    kernel(*refs)


def call(kernel, out_shape, args, scratch=(), held=(), mib=24):
    specs = [SMEM] + [HBM if i in held else VMEM for i in range(1, len(args))]
    scratch = list(scratch)
    if held:
        kernel = functools.partial(fetching, kernel, tuple(held))
        scratch += [pltpu.VMEM(args[i].shape, args[i].dtype) for i in held]
        scratch += [pltpu.SemaphoreType.DMA((len(held),))]
    return pl.pallas_call(
        kernel,
        out_shape=out_shape,
        in_specs=specs,
        out_specs=jax.tree.map(lambda _: VMEM, out_shape),
        scratch_shapes=scratch,
        compiler_params=pltpu.CompilerParams(vmem_limit_bytes=mib * 2**20),
        cost_estimate=TINY,
    )(*args)


PARTS = 7


def factor(packs, i):
    feats = packs.shape[2] // PARTS
    return packs[:, :, i * feats : (i + 1) * feats].reshape(NH * RANK, feats)


def factors_kernel(pos, early, early_sib, up_q, up_kv, down_o, up_o):
    feats = up_o.shape[1]
    up_q[:, :feats] = factor(early, 3)
    up_q[:, feats:] = factor(early_sib, 3)
    up_kv[...] = factor(early, 4)
    down_o[:, :feats] = factor(early, 5)
    down_o[:, feats:] = factor(early_sib, 5)
    up_o[...] = factor(early, 6)


def kv_kernel(pos, tokens, tok_sib, wk, wv, wk_sib, wv_sib, own, s1, s2, s3, both):
    x, c = pos[1], pos[3]
    half, width = tok_sib.shape[0], wk.shape[1]
    mine = tokens[at(c * half, half), :]
    for i, (w, w_sib) in enumerate(((wk, wk_sib), (wv, wv_sib))):
        part = dot(mine, w[...]) + dot(tok_sib[...], w_sib[...])
        for g in range(width // HEAD_DIM):
            base = ((g % 2) * NZ * 2 + (g // 2) * 2 + i) * HEAD_DIM
            both[:, base : base + HEAD_DIM] = part[:, g * HEAD_DIM : (g + 1) * HEAD_DIM]
    for d, out in enumerate((own, s1, s2, s3)):
        xh = lax.rem(x + NX - d, NX) // 2
        out[...] = both[:, at(xh * width, width)].astype(out.dtype)


def kv_middle_kernel(pos, a0, a1, a2, a3, own, s1, s2, s3):
    z = pos[2]
    width = own.shape[1]
    for d, out in enumerate((own, s1, s2, s3)):
        cols = at(lax.rem(z + NZ - d, NZ) * width, width)
        total = a0[:, cols] + a1[:, cols].astype(F32)
        total = total + a2[:, cols].astype(F32) + a3[:, cols].astype(F32)
        out[...] = total.astype(out.dtype)


def rank_kernel(pos, tokens, packs, mine, send, stack):
    c = pos[3]
    half = mine.shape[0]
    feats = tokens.shape[1]
    for d in range(NH):
        for p in range(3):
            row = (p * NH + d) * RANK
            stack[row : row + RANK, :] = packs[d, :, p * feats : (p + 1) * feats]
    mine[...] = dot_t(tokens[at(c * half, half), :], stack[...])
    send[...] = dot_t(tokens[at((1 - c) * half, half), :], stack[...]).astype(BF)


def rank_split_kernel(pos, mine, recv, out):
    out[...] = (mine[...] + recv[...].astype(F32)).reshape(out.shape).astype(BF)


def rank_sum_kernel(pos, parts, out):
    total = parts[0].astype(F32)
    for i in range(1, NZ * NX):
        total = total + parts[i].astype(F32)
    for i in range(NZ * NX):
        out[i] = total.astype(BF)


def gather_ranks(pieces, cols):
    chips, rows, _ = pieces.shape
    part = pieces[:, :, cols].astype(F32)
    return part.reshape(chips * rows, part.shape[2]).astype(BF)


def kv_final_kernel(pos, pieces, a0, a1, a2, a3, up, out):
    n = NH * RANK
    kv = a0[...] + a1[...].astype(F32) + a2[...].astype(F32) + a3[...].astype(F32)
    low_k = dot(gather_ranks(pieces, slice(n, 2 * n)), up[:, :HEAD_DIM])
    low_v = dot(gather_ranks(pieces, slice(2 * n, 3 * n)), up[:, HEAD_DIM:])
    out[:, :HEAD_DIM] = (kv[:, :HEAD_DIM] + low_k * SCALE).astype(BF)
    out[:, HEAD_DIM:] = (kv[:, HEAD_DIM:] + low_v * SCALE).astype(BF)


def attend_kernel(pos, pieces, q_mine, q_recv, up_q, kv_mine, kv_recv, out, kv, q):
    c = pos[3]
    half, feats = q_mine.shape
    low = dot(gather_ranks(pieces, slice(0, NH * RANK)), up_q[...]) * SCALE
    q[:, :feats] = (q_mine[...] + low[:, :feats]).astype(BF)
    q[:, feats:] = (q_recv[...] + low[:, feats:]).astype(BF)
    kv[at(c * half, half), :] = kv_mine[...]
    kv[at((1 - c) * half, half), :] = kv_recv[...]
    k, v = kv[:, :HEAD_DIM], kv[:, HEAD_DIM:]
    rows = lax.broadcasted_iota(jnp.int32, (half, 2 * half), 0) + c * half
    causal = rows >= lax.broadcasted_iota(jnp.int32, (half, 2 * half), 1)
    for head in range(2 * feats // HEAD_DIM):
        cols = slice(head * HEAD_DIM, (head + 1) * HEAD_DIM)
        scores = dot_t(q[:, cols], k) * (1.0 / math.sqrt(HEAD_DIM))
        scores = jnp.where(causal, scores, -jnp.inf)
        weights = jnp.exp(scores - jnp.max(scores, axis=-1, keepdims=True))
        probs = (weights / jnp.sum(weights, axis=-1, keepdims=True)).astype(BF)
        out[:, cols] = dot(probs, v).astype(BF)


def query_kernel(pos, tok, w, mine, send, total):
    c = pos[3]
    step = pl.program_id(0)

    @pl.when(step == 0)
    def _():
        total[...] = jnp.zeros_like(total)

    part = dot(tok[0], w[0])
    for i in range(1, tok.shape[0]):
        part = part + dot(tok[i], w[i])
    total[...] += part

    @pl.when(step == pl.num_programs(0) - 1)
    def _():
        half = mine.shape[0]
        mine[...] = total[at(c * half, half), :]
        send[...] = total[at((1 - c) * half, half), :]


def query(pos, toks, w_query):
    blocks, rows, feats = toks.shape
    half = rows // NC
    steps = 4
    part = pl.BlockSpec((blocks // steps, rows, feats), lambda d, pos: (d, 0, 0))
    return pl.pallas_call(
        query_kernel,
        grid_spec=pltpu.PrefetchScalarGridSpec(
            num_scalar_prefetch=1,
            grid=(steps,),
            in_specs=[part, part],
            out_specs=[pl.BlockSpec((half, feats), lambda d, pos: (0, 0))] * 2,
            scratch_shapes=[pltpu.VMEM((rows, feats), F32)],
        ),
        out_shape=[struct((half, feats), F32)] * 2,
        compiler_params=pltpu.CompilerParams(vmem_limit_bytes=40 * 2**20),
        cost_estimate=TINY,
    )(pos, toks, w_query)


SPLIT = 4


def out_kernel(pos, att, att_recv, w, w_sib, out, rows_in, here, done, sem, out_sem):
    z, c = pos[2], pos[3]
    rows, feats = done.shape[1:]
    blocks = done.shape[0]
    half = rows // NC
    pairs = blocks // 2

    for k in range(blocks):
        cols = at((NC * k + c) * feats, feats)
        to = slice(k % 2 * feats, (k % 2 + 1) * feats)
        for i, a in enumerate((w, w_sib)):
            for j in range(SPLIT):
                part = slice(j * feats // SPLIT, (j + 1) * feats // SPLIT)
                place = slice(i * feats + part.start, i * feats + part.stop)
                pltpu.make_async_copy(
                    a.at[part, cols], here.at[k // 2, place, to], sem.at[2 * k + i]
                ).start()
    rows_in[at(c * half, half), :] = att[...]
    other = at((1 - c) * half, half)
    rows_in[other, :feats] = att_recv[:, feats:]
    rows_in[other, feats:] = att_recv[:, :feats]

    def leave(k):
        place = out.at[k % NX, lax.rem(k // NX + NZ - z, NZ)]
        return pltpu.make_async_copy(done.at[k], place, out_sem.at[k])

    for p in range(pairs):
        for k in (2 * p, 2 * p + 1):
            for i in range(2):
                part = here.at[p, i * feats : (i + 1) * feats, k % 2 * feats : (k % 2 + 1) * feats]
                pltpu.make_async_copy(w.at[:, :feats], part, sem.at[2 * k + i]).wait()
        both = dot(rows_in[...], here[p]).astype(BF)
        for k in (2 * p, 2 * p + 1):
            done[k] = both[:, k % 2 * feats : (k % 2 + 1) * feats]
            leave(k).start()
    for k in range(blocks):
        leave(k).wait()


def out_partial(pos, att, att_recv, w_out, w_sib):
    half, width = att.shape
    feats = width // NC
    rows = NC * half
    blocks = NX * NZ
    return pl.pallas_call(
        out_kernel,
        in_specs=[SMEM, VMEM, VMEM, HBM, HBM],
        out_specs=HBM,
        out_shape=struct((NX, NZ, rows, feats), BF),
        scratch_shapes=[
            pltpu.VMEM((rows, width), BF),
            pltpu.VMEM((blocks // 2, width, 2 * feats), BF),
            pltpu.VMEM((blocks, rows, feats), BF),
            pltpu.SemaphoreType.DMA((2 * blocks,)),
            pltpu.SemaphoreType.DMA((blocks,)),
        ],
        compiler_params=pltpu.CompilerParams(vmem_limit_bytes=50 * 2**20),
        cost_estimate=TINY,
    )(pos, att, att_recv, w_out, w_sib)


def out_rank_kernel(pos, att, down_o, out):
    out[...] = dot_t(att[...], down_o[...]).astype(BF)


def add_kernel(pos, a0, a1, a2, a3, out):
    total = a0[...].astype(F32) + a1[...].astype(F32)
    out[...] = (total + a2[...].astype(F32) + a3[...].astype(F32)).astype(BF)


def rank_rows_kernel(pos, a0, a1, a2, a3, own, s1, s2, s3, total):
    total[...] = a0[...].astype(F32) + a1[...].astype(F32) + a2[...].astype(F32) + a3[...].astype(F32)
    part = own.shape[0]
    for d, out in enumerate((own, s1, s2, s3)):
        rows = at(lax.rem(pos[1] + NX - d, NX) * part, part, part)
        out[...] = total[rows, :].astype(BF)


def rank_join_kernel(pos, a0, a1, a2, a3, out):
    part = a0.shape[0]
    for d, a in enumerate((a0, a1, a2, a3)):
        out[at(lax.rem(pos[1] + d, NX) * part, part, part), :] = a[...]


def final_kernel(pos, a0, a1, a2, a3, rank, rank_recv, up_o, out):
    c = pos[3]
    half = rank.shape[0]
    for part, start in ((rank, c * half), (rank_recv, (1 - c) * half)):
        rows = at(start, half)
        total = a0[rows, :].astype(F32) + a1[rows, :].astype(F32)
        total = total + a2[rows, :].astype(F32) + a3[rows, :].astype(F32)
        out[rows, :] = (total + dot(part[...], up_o[...]) * SCALE).astype(BF)


def body(
    tokens,
    w_query,
    w_key,
    w_value,
    w_out,
    down_query,
    up_query,
    down_key,
    up_key,
    down_value,
    up_value,
    down_out,
    up_out,
):
    h = lax.axis_index("head")
    t = lax.axis_index("tensor")
    c = t % NC
    x = (t // NC) % NX
    z = t // (NX * NC)
    pos = jnp.stack([h, x, z, c]).astype(jnp.int32)
    rows, feats = tokens.shape
    half = rows // NC
    n = NH * RANK
    vm = pltpu.VMEM
    x_groups = tensor_groups(lambda z, x, c: (z, c))

    def four(shape):
        return [struct(shape, F32)] + [struct(shape, BF)] * 3

    tok_zs = [tokens] + [from_z(tokens, d) for d in (1, 2, 3)]
    g = t // 4
    downs = [jnp.swapaxes(a, 1, 2) for a in (down_query, down_key, down_value, down_out)]
    up_kv = [lax.dynamic_slice_in_dim(a, g * HEAD_DIM, HEAD_DIM, 2) for a in (up_key, up_value)]
    early = join([*downs[:3], up_query, *up_kv, downs[3], up_out])
    early = swap_all(jnp.broadcast_to(early, (NH, *early.shape[1:])), "head")

    tok_all = lax.all_gather(tokens[None], "tensor", axis=0, tiled=True)

    tok_sib = from_core(lax.dynamic_slice_in_dim(tokens, (1 - c) * half, half, 0))
    own, *sends = call(
        kv_kernel,
        four((half, NZ * 2 * HEAD_DIM)),
        (pos, tokens, tok_sib, w_key, w_value, from_core(w_key), from_core(w_value)),
        [vm((half, 2 * w_key.shape[1]), F32)],
        held=(1, 3, 4),
    )
    kv_x = [own] + [from_x(s, d) for d, s in zip((1, 2, 3), sends)]
    early, kv_x = tie(early, kv_x)

    mine, send = call(
        rank_kernel,
        [struct((half, 3 * n), F32), struct((half, 3 * n), BF)],
        (pos, tokens, early),
        [vm((3 * n, feats), BF)],
        held=(1,),
    )
    chips = NZ * NX
    pieces = call(
        rank_split_kernel,
        struct((chips, half // chips, 3 * n), BF),
        (pos, mine, from_core(send)),
    )
    early_sib = from_core(early)
    own, *sends = call(kv_middle_kernel, four((half, 2 * HEAD_DIM)), (pos, *kv_x))
    kv_z = [own] + [from_z(s, d) for d, s in zip((1, 2, 3), sends)]
    pieces = swap_xz(pieces)
    factors = call(
        factors_kernel,
        [
            struct((n, NC * feats), BF),
            struct((n, feats), BF),
            struct((n, NC * feats), BF),
            struct((n, feats), BF),
        ],
        (pos, early, early_sib),
    )
    pieces, factors, w_out_now, kv_z = tie(pieces, factors, w_out, kv_z)
    up_q, up_kv, down_o, up_o = factors
    w_o_sib = from_core(w_out_now)
    pieces = call(rank_sum_kernel, struct(pieces.shape, BF), (pos, pieces))
    pieces = swap_xz(pieces)

    q_mine, q_send = query(pos, tok_all, w_query.reshape(NZ * NX * NC, feats, feats))
    q_recv = from_core(q_send)
    pieces, w_o_sib, q_recv = tie(pieces, w_o_sib, q_recv)
    kv_mine = call(kv_final_kernel, struct((half, 2 * HEAD_DIM), BF), (pos, pieces, *kv_z, up_kv))

    att = call(
        attend_kernel,
        struct((half, NC * feats), BF),
        (pos, pieces, q_mine, q_recv, up_q, kv_mine, from_core(kv_mine)),
        [vm((rows, 2 * HEAD_DIM), BF), vm((half, NC * feats), BF)],
    )

    rank_o = call(out_rank_kernel, struct((half, n), BF), (pos, att, down_o))
    att, rank_o = tie(att, rank_o)
    out = out_partial(pos, att, from_core(att), w_out, w_o_sib)
    out_x = lax.psum_scatter(
        out, "tensor", scatter_dimension=0, tiled=True, axis_index_groups=x_groups
    )
    own, *sends = call(
        rank_rows_kernel,
        [struct((half // NX, n), BF)] * NX,
        (pos, rank_o, *[from_z(rank_o, d) for d in (1, 2, 3)]),
        [vm((half, n), F32)],
    )
    part = call(
        add_kernel,
        struct((half // NX, n), BF),
        (pos, own, *[from_x(s, d) for d, s in zip((1, 2, 3), sends)]),
    )
    rank_o = call(
        rank_join_kernel,
        struct((half, n), BF),
        (pos, part, *[from_x(part, d) for d in (1, 2, 3)]),
    )
    out_x = [out_x[0, i] for i in range(NZ)]
    out_z = [out_x[0]] + [from_z(out_x[NZ - d], d) for d in (1, 2, 3)]
    return call(
        final_kernel,
        struct((rows, feats), BF),
        (pos, *out_z, rank_o, from_core(rank_o), up_o),
    )


def solution(mesh):
    placed = (
        P("head", "tensor"),
        P(None, "tensor"),
        P("tensor", None),
        P("tensor", None),
        P("tensor", None),
        P("head", "tensor", None),
        P("head", None, "tensor"),
        P("head", "tensor", None),
        P("head", None, None),
        P("head", "tensor", None),
        P("head", None, None),
        P("head", "tensor", None),
        P("head", None, "tensor"),
    )
    return jax.shard_map(
        body, mesh=mesh, in_specs=placed, out_specs=P("head", "tensor"), check_vma=False
    )
```

```python
import functools
import math

import jax
import jax.numpy as jnp
from jax import lax
from jax.experimental import pallas as pl
from jax.experimental.pallas import tpu as pltpu
from jax.sharding import PartitionSpec as P

HEAD_DIM = 128
ADAPTER_SCALE = 2.0
NZ, NX, NC = 4, 4, 2
NH = 8
RANK = 64
SCALE = ADAPTER_SCALE / NH
BF = jnp.bfloat16
F32 = jnp.float32
VMEM = pl.BlockSpec(memory_space=pltpu.VMEM)
HBM = pl.BlockSpec(memory_space=pltpu.HBM)
TINY = pl.CostEstimate(flops=1000, bytes_accessed=1000, transcendentals=0)
SMEM = pl.BlockSpec(memory_space=pltpu.SMEM)


def tensor_perm(dz, dx, dc):
    pairs = []
    for t in range(NZ * NX * NC):
        z, x, c = t // (NX * NC), (t // NC) % NX, t % NC
        to = (((z - dz) % NZ) * NX + (x - dx) % NX) * NC + (c ^ dc)
        pairs.append((t, to))
    return pairs


def from_core(a):
    return lax.ppermute(a, "tensor", tensor_perm(0, 0, 1))


def from_x(a, d):
    return lax.ppermute(a, "tensor", tensor_perm(0, d, 0))


def from_z(a, d):
    return lax.ppermute(a, "tensor", tensor_perm(d, 0, 0))


def from_head(a, d):
    return lax.ppermute(a, "head", [(h, (h - d) % NH) for h in range(NH)])


def swap_all(a, axis, groups=None):
    return lax.all_to_all(a, axis, 0, 0, axis_index_groups=groups, tiled=True)


def tensor_groups(key):
    groups = {}
    for t in range(NZ * NX * NC):
        groups.setdefault(key(t // (NX * NC), (t // NC) % NX, t % NC), []).append(t)
    return list(groups.values())


def swap_x(a):
    return swap_all(a, "tensor", tensor_groups(lambda z, x, c: (z, c)))


def swap_z(a):
    return swap_all(a, "tensor", tensor_groups(lambda z, x, c: (x, c)))


def swap_xz(a):
    return swap_all(a, "tensor", tensor_groups(lambda z, x, c: c))


def dot(a, b):
    return jnp.dot(a, b, preferred_element_type=F32)


def dot_t(a, b):
    return lax.dot_general(a, b, (((1,), (1,)), ((), ())), preferred_element_type=F32)


def join(parts):
    width = sum(a.shape[-1] for a in parts)
    total, start = None, 0
    for a in parts:
        edges = [(0, 0, 0)] * (a.ndim - 1) + [(start, width - start - a.shape[-1], 0)]
        piece = lax.pad(a, jnp.zeros((), a.dtype), edges)
        total = piece if total is None else total + piece
        start += a.shape[-1]
    return total


def tie(*parts):
    return lax.optimization_barrier(parts)


def at(start, size, unit=128):
    return pl.ds(pl.multiple_of(start, unit), size)


def struct(shape, dtype):
    return jax.ShapeDtypeStruct(shape, dtype)


def fetching(kernel, held, *refs):
    refs, extra = list(refs[:-len(held) - 1]), refs[-len(held) - 1 :]
    buffers, sem = extra[:-1], extra[-1]
    copies = [
        pltpu.make_async_copy(refs[place], buffer, sem.at[i])
        for i, (place, buffer) in enumerate(zip(held, buffers))
    ]
    for copy in copies:
        copy.start()
    for copy in copies:
        copy.wait()
    for place, buffer in zip(held, buffers):
        refs[place] = buffer
    kernel(*refs)


def call(kernel, out_shape, args, scratch=(), held=(), mib=24):
    specs = [SMEM] + [HBM if i in held else VMEM for i in range(1, len(args))]
    scratch = list(scratch)
    if held:
        kernel = functools.partial(fetching, kernel, tuple(held))
        scratch += [pltpu.VMEM(args[i].shape, args[i].dtype) for i in held]
        scratch += [pltpu.SemaphoreType.DMA((len(held),))]
    return pl.pallas_call(
        kernel,
        out_shape=out_shape,
        in_specs=specs,
        out_specs=jax.tree.map(lambda _: VMEM, out_shape),
        scratch_shapes=scratch,
        compiler_params=pltpu.CompilerParams(vmem_limit_bytes=mib * 2**20),
        cost_estimate=TINY,
    )(*args)


PARTS = 7


def factor(packs, i):
    feats = packs.shape[2] // PARTS
    return packs[:, :, i * feats : (i + 1) * feats].reshape(NH * RANK, feats)


def factors_kernel(pos, early, early_sib, up_q, up_kv, down_o, up_o):
    feats = up_o.shape[1]
    up_q[:, :feats] = factor(early, 3)
    up_q[:, feats:] = factor(early_sib, 3)
    up_kv[...] = factor(early, 4)
    down_o[:, :feats] = factor(early, 5)
    down_o[:, feats:] = factor(early_sib, 5)
    up_o[...] = factor(early, 6)


def kv_kernel(pos, tokens, tok_sib, wk, wv, wk_sib, wv_sib, own, s1, s2, s3, both):
    x, c = pos[1], pos[3]
    half, width = tok_sib.shape[0], wk.shape[1]
    mine = tokens[at(c * half, half), :]
    for i, (w, w_sib) in enumerate(((wk, wk_sib), (wv, wv_sib))):
        part = dot(mine, w[...]) + dot(tok_sib[...], w_sib[...])
        for g in range(width // HEAD_DIM):
            base = ((g % 2) * NZ * 2 + (g // 2) * 2 + i) * HEAD_DIM
            both[:, base : base + HEAD_DIM] = part[:, g * HEAD_DIM : (g + 1) * HEAD_DIM]
    for d, out in enumerate((own, s1, s2, s3)):
        xh = lax.rem(x + NX - d, NX) // 2
        out[...] = both[:, at(xh * width, width)].astype(out.dtype)


def kv_middle_kernel(pos, a0, a1, a2, a3, own, s1, s2, s3):
    z = pos[2]
    width = own.shape[1]
    for d, out in enumerate((own, s1, s2, s3)):
        cols = at(lax.rem(z + NZ - d, NZ) * width, width)
        total = a0[:, cols] + a1[:, cols].astype(F32)
        total = total + a2[:, cols].astype(F32) + a3[:, cols].astype(F32)
        out[...] = total.astype(out.dtype)


def rank_kernel(pos, tokens, packs, mine, send, stack):
    c = pos[3]
    half = mine.shape[0]
    feats = tokens.shape[1]
    for d in range(NH):
        for p in range(3):
            row = (p * NH + d) * RANK
            stack[row : row + RANK, :] = packs[d, :, p * feats : (p + 1) * feats]
    mine[...] = dot_t(tokens[at(c * half, half), :], stack[...])
    send[...] = dot_t(tokens[at((1 - c) * half, half), :], stack[...]).astype(BF)


def rank_split_kernel(pos, mine, recv, out):
    out[...] = (mine[...] + recv[...].astype(F32)).reshape(out.shape).astype(BF)


def rank_sum_kernel(pos, parts, out):
    total = parts[0].astype(F32)
    for i in range(1, NZ * NX):
        total = total + parts[i].astype(F32)
    for i in range(NZ * NX):
        out[i] = total.astype(BF)


def gather_ranks(pieces, cols):
    chips, rows, _ = pieces.shape
    part = pieces[:, :, cols].astype(F32)
    return part.reshape(chips * rows, part.shape[2]).astype(BF)


def kv_final_kernel(pos, pieces, a0, a1, a2, a3, up, out):
    n = NH * RANK
    kv = a0[...] + a1[...].astype(F32) + a2[...].astype(F32) + a3[...].astype(F32)
    low_k = dot(gather_ranks(pieces, slice(n, 2 * n)), up[:, :HEAD_DIM])
    low_v = dot(gather_ranks(pieces, slice(2 * n, 3 * n)), up[:, HEAD_DIM:])
    out[:, :HEAD_DIM] = (kv[:, :HEAD_DIM] + low_k * SCALE).astype(BF)
    out[:, HEAD_DIM:] = (kv[:, HEAD_DIM:] + low_v * SCALE).astype(BF)


def attend_kernel(pos, pieces, q_mine, q_recv, up_q, kv_mine, kv_recv, out, kv, q):
    c = pos[3]
    half, feats = q_mine.shape
    low = dot(gather_ranks(pieces, slice(0, NH * RANK)), up_q[...]) * SCALE
    q[:, :feats] = (q_mine[...] + low[:, :feats]).astype(BF)
    q[:, feats:] = (q_recv[...] + low[:, feats:]).astype(BF)
    kv[at(c * half, half), :] = kv_mine[...]
    kv[at((1 - c) * half, half), :] = kv_recv[...]
    k, v = kv[:, :HEAD_DIM], kv[:, HEAD_DIM:]
    rows = lax.broadcasted_iota(jnp.int32, (half, 2 * half), 0) + c * half
    causal = rows >= lax.broadcasted_iota(jnp.int32, (half, 2 * half), 1)
    for head in range(2 * feats // HEAD_DIM):
        cols = slice(head * HEAD_DIM, (head + 1) * HEAD_DIM)
        scores = dot_t(q[:, cols], k) * (1.0 / math.sqrt(HEAD_DIM))
        scores = jnp.where(causal, scores, -jnp.inf)
        weights = jnp.exp(scores - jnp.max(scores, axis=-1, keepdims=True))
        probs = (weights / jnp.sum(weights, axis=-1, keepdims=True)).astype(BF)
        out[:, cols] = dot(probs, v).astype(BF)


def query_kernel(pos, tok, w, mine, send, total):
    c = pos[3]
    step = pl.program_id(0)

    @pl.when(step == 0)
    def _():
        total[...] = jnp.zeros_like(total)

    part = dot(tok[0], w[0])
    for i in range(1, tok.shape[0]):
        part = part + dot(tok[i], w[i])
    total[...] += part

    @pl.when(step == pl.num_programs(0) - 1)
    def _():
        half = mine.shape[0]
        mine[...] = total[at(c * half, half), :]
        send[...] = total[at((1 - c) * half, half), :]


def query(pos, toks, w_query):
    blocks, rows, feats = toks.shape
    half = rows // NC
    steps = 4
    part = pl.BlockSpec((blocks // steps, rows, feats), lambda d, pos: (d, 0, 0))
    return pl.pallas_call(
        query_kernel,
        grid_spec=pltpu.PrefetchScalarGridSpec(
            num_scalar_prefetch=1,
            grid=(steps,),
            in_specs=[part, part],
            out_specs=[pl.BlockSpec((half, feats), lambda d, pos: (0, 0))] * 2,
            scratch_shapes=[pltpu.VMEM((rows, feats), F32)],
        ),
        out_shape=[struct((half, feats), F32)] * 2,
        compiler_params=pltpu.CompilerParams(vmem_limit_bytes=40 * 2**20),
        cost_estimate=TINY,
    )(pos, toks, w_query)


SPLIT = 4


def out_kernel(pos, att, att_recv, w, w_sib, out, rows_in, here, done, sem, out_sem):
    z, c = pos[2], pos[3]
    rows, feats = done.shape[1:]
    blocks = done.shape[0]
    half = rows // NC
    pairs = blocks // 2

    for k in range(blocks):
        cols = at((NC * k + c) * feats, feats)
        to = slice(k % 2 * feats, (k % 2 + 1) * feats)
        for i, a in enumerate((w, w_sib)):
            for j in range(SPLIT):
                part = slice(j * feats // SPLIT, (j + 1) * feats // SPLIT)
                place = slice(i * feats + part.start, i * feats + part.stop)
                pltpu.make_async_copy(
                    a.at[part, cols], here.at[k // 2, place, to], sem.at[2 * k + i]
                ).start()
    rows_in[at(c * half, half), :] = att[...]
    other = at((1 - c) * half, half)
    rows_in[other, :feats] = att_recv[:, feats:]
    rows_in[other, feats:] = att_recv[:, :feats]

    def leave(k):
        place = out.at[k % NX, lax.rem(k // NX + NZ - z, NZ)]
        return pltpu.make_async_copy(done.at[k], place, out_sem.at[k])

    for p in range(pairs):
        for k in (2 * p, 2 * p + 1):
            for i in range(2):
                part = here.at[p, i * feats : (i + 1) * feats, k % 2 * feats : (k % 2 + 1) * feats]
                pltpu.make_async_copy(w.at[:, :feats], part, sem.at[2 * k + i]).wait()
        both = dot(rows_in[...], here[p]).astype(BF)
        for k in (2 * p, 2 * p + 1):
            done[k] = both[:, k % 2 * feats : (k % 2 + 1) * feats]
            leave(k).start()
    for k in range(blocks):
        leave(k).wait()


def out_partial(pos, att, att_recv, w_out, w_sib):
    half, width = att.shape
    feats = width // NC
    rows = NC * half
    blocks = NX * NZ
    return pl.pallas_call(
        out_kernel,
        in_specs=[SMEM, VMEM, VMEM, HBM, HBM],
        out_specs=HBM,
        out_shape=struct((NX, NZ, rows, feats), BF),
        scratch_shapes=[
            pltpu.VMEM((rows, width), BF),
            pltpu.VMEM((blocks // 2, width, 2 * feats), BF),
            pltpu.VMEM((blocks, rows, feats), BF),
            pltpu.SemaphoreType.DMA((2 * blocks,)),
            pltpu.SemaphoreType.DMA((blocks,)),
        ],
        compiler_params=pltpu.CompilerParams(vmem_limit_bytes=50 * 2**20),
        cost_estimate=TINY,
    )(pos, att, att_recv, w_out, w_sib)


def out_rank_kernel(pos, att, down_o, out):
    out[...] = dot_t(att[...], down_o[...]).astype(BF)


def add_kernel(pos, a0, a1, a2, a3, out):
    total = a0[...].astype(F32) + a1[...].astype(F32)
    out[...] = (total + a2[...].astype(F32) + a3[...].astype(F32)).astype(BF)


def rank_rows_kernel(pos, a0, a1, a2, a3, own, s1, s2, s3, total):
    total[...] = a0[...].astype(F32) + a1[...].astype(F32) + a2[...].astype(F32) + a3[...].astype(F32)
    part = own.shape[0]
    for d, out in enumerate((own, s1, s2, s3)):
        rows = at(lax.rem(pos[1] + NX - d, NX) * part, part, part)
        out[...] = total[rows, :].astype(BF)


def rank_join_kernel(pos, a0, a1, a2, a3, out):
    part = a0.shape[0]
    for d, a in enumerate((a0, a1, a2, a3)):
        out[at(lax.rem(pos[1] + d, NX) * part, part, part), :] = a[...]


def final_kernel(pos, a0, a1, a2, a3, rank, rank_recv, up_o, out):
    c = pos[3]
    half = rank.shape[0]
    for part, start in ((rank, c * half), (rank_recv, (1 - c) * half)):
        rows = at(start, half)
        total = a0[rows, :].astype(F32) + a1[rows, :].astype(F32)
        total = total + a2[rows, :].astype(F32) + a3[rows, :].astype(F32)
        out[rows, :] = (total + dot(part[...], up_o[...]) * SCALE).astype(BF)


def body(
    tokens,
    w_query,
    w_key,
    w_value,
    w_out,
    down_query,
    up_query,
    down_key,
    up_key,
    down_value,
    up_value,
    down_out,
    up_out,
):
    h = lax.axis_index("head")
    t = lax.axis_index("tensor")
    c = t % NC
    x = (t // NC) % NX
    z = t // (NX * NC)
    pos = jnp.stack([h, x, z, c]).astype(jnp.int32)
    rows, feats = tokens.shape
    half = rows // NC
    n = NH * RANK
    vm = pltpu.VMEM
    x_groups = tensor_groups(lambda z, x, c: (z, c))

    def four(shape):
        return [struct(shape, F32)] + [struct(shape, BF)] * 3

    tok_zs = [tokens] + [from_z(tokens, d) for d in (1, 2, 3)]
    g = t // 4
    downs = [jnp.swapaxes(a, 1, 2) for a in (down_query, down_key, down_value, down_out)]
    up_kv = [lax.dynamic_slice_in_dim(a, g * HEAD_DIM, HEAD_DIM, 2) for a in (up_key, up_value)]
    early = join([*downs[:3], up_query, *up_kv, downs[3], up_out])
    early = swap_all(jnp.broadcast_to(early, (NH, *early.shape[1:])), "head")

    tok_all = lax.all_gather(tokens[None], "tensor", axis=0, tiled=True)

    tok_sib = from_core(lax.dynamic_slice_in_dim(tokens, (1 - c) * half, half, 0))
    own, *sends = call(
        kv_kernel,
        four((half, NZ * 2 * HEAD_DIM)),
        (pos, tokens, tok_sib, w_key, w_value, from_core(w_key), from_core(w_value)),
        [vm((half, 2 * w_key.shape[1]), F32)],
        held=(1, 3, 4),
    )
    kv_x = [own] + [from_x(s, d) for d, s in zip((1, 2, 3), sends)]
    early, kv_x[0] = tie(early, kv_x[0])

    mine, send = call(
        rank_kernel,
        [struct((half, 3 * n), F32), struct((half, 3 * n), BF)],
        (pos, tokens, early),
        [vm((3 * n, feats), BF)],
        held=(1,),
    )
    chips = NZ * NX
    pieces = call(
        rank_split_kernel,
        struct((chips, half // chips, 3 * n), BF),
        (pos, mine, from_core(send)),
    )
    early_sib = from_core(early)
    pieces, kv_x = tie(pieces, kv_x)
    own, *sends = call(kv_middle_kernel, four((half, 2 * HEAD_DIM)), (pos, *kv_x))
    kv_z = [own] + [from_z(s, d) for d, s in zip((1, 2, 3), sends)]
    pieces = swap_xz(pieces)
    factors = call(
        factors_kernel,
        [
            struct((n, NC * feats), BF),
            struct((n, feats), BF),
            struct((n, NC * feats), BF),
            struct((n, feats), BF),
        ],
        (pos, early, early_sib),
    )
    pieces, factors, w_out_now, kv_z = tie(pieces, factors, w_out, kv_z)
    up_q, up_kv, down_o, up_o = factors
    w_o_sib = from_core(w_out_now)
    pieces = call(rank_sum_kernel, struct(pieces.shape, BF), (pos, pieces))
    pieces = swap_xz(pieces)

    q_mine, q_send = query(pos, tok_all, w_query.reshape(NZ * NX * NC, feats, feats))
    q_recv = from_core(q_send)
    pieces, w_o_sib, q_recv = tie(pieces, w_o_sib, q_recv)
    kv_mine = call(kv_final_kernel, struct((half, 2 * HEAD_DIM), BF), (pos, pieces, *kv_z, up_kv))

    att = call(
        attend_kernel,
        struct((half, NC * feats), BF),
        (pos, pieces, q_mine, q_recv, up_q, kv_mine, from_core(kv_mine)),
        [vm((rows, 2 * HEAD_DIM), BF), vm((half, NC * feats), BF)],
    )

    rank_o = call(out_rank_kernel, struct((half, n), BF), (pos, att, down_o))
    att, rank_o = tie(att, rank_o)
    out = out_partial(pos, att, from_core(att), w_out, w_o_sib)
    out_x = lax.psum_scatter(
        out, "tensor", scatter_dimension=0, tiled=True, axis_index_groups=x_groups
    )
    own, *sends = call(
        rank_rows_kernel,
        [struct((half // NX, n), BF)] * NX,
        (pos, rank_o, *[from_z(rank_o, d) for d in (1, 2, 3)]),
        [vm((half, n), F32)],
    )
    part = call(
        add_kernel,
        struct((half // NX, n), BF),
        (pos, own, *[from_x(s, d) for d, s in zip((1, 2, 3), sends)]),
    )
    rank_o = call(
        rank_join_kernel,
        struct((half, n), BF),
        (pos, part, *[from_x(part, d) for d in (1, 2, 3)]),
    )
    out_x = [out_x[0, i] for i in range(NZ)]
    out_z = [out_x[0]] + [from_z(out_x[NZ - d], d) for d in (1, 2, 3)]
    return call(
        final_kernel,
        struct((rows, feats), BF),
        (pos, *out_z, rank_o, from_core(rank_o), up_o),
    )


def solution(mesh):
    placed = (
        P("head", "tensor"),
        P(None, "tensor"),
        P("tensor", None),
        P("tensor", None),
        P("tensor", None),
        P("head", "tensor", None),
        P("head", None, "tensor"),
        P("head", "tensor", None),
        P("head", None, None),
        P("head", "tensor", None),
        P("head", None, None),
        P("head", "tensor", None),
        P("head", None, "tensor"),
    )
    return jax.shard_map(
        body, mesh=mesh, in_specs=placed, out_specs=P("head", "tensor"), check_vma=False
    )
```
